256 devices in a mesh: ctx: 64 (over y, z, core), head: 4 (over x).
Axes of the slice: x: 4, y: 4, z: 8, core: 2. Of those that a mesh axis runs over, the one named last changes fastest.
Arguments:
- query_nope: bfloat16 [2, 32, 8192], P(None, None, 'head'), may hold values from -12 to 12
- query_rope: bfloat16 [2, 32, 4096], P(None, None, 'head'), may hold values from -9 to 9
- key_up: bfloat16 [64, 128, 512], P('head'), may hold values from -0.5 to 0.5
- cache_latent: bfloat16 [131072, 512], P('ctx'), may hold values from -6 to 6
- cache_rope: bfloat16 [65536, 128], P('ctx'), may hold values from -6 to 6
- chosen_blocks: int32 [2, 32, 16], replicated, may hold values from 0 to 1023, as said below
- value_up: bfloat16 [64, 512, 128], P('head', 'ctx'), may hold values from -0.25 to 0.25
- output_weight: bfloat16 [8192, 7168], P('head', 'ctx'), may hold values from -0.25 to 0.25
Outputs:
- attention_out: bfloat16 [2, 32, 7168], P(None, 'head', 'ctx')
The draws below stay inside these ranges and needn't reach their ends.
Inputs may be any that keep to these rules, and one draw needn't show every extreme that they name: `chosen_blocks`: each row names 16 different blocks at each step. In each step, the blocks i * 16 to (i + 1) * 16 - 1 are named at most 24 times over all rows, and exactly 24 times for some i.
All inputs are finite; a program needn't handle non-finite values.
Results may differ from the reference program's by a relative error of at most 0.0078.
Values may be sent and summed in bfloat16 or wider, within the bound.
No kernel may reach another device: no remote copies, remote signals or barrier semaphores. Data moves between devices by JAX's collectives and lax.ppermute only.
A program may use at most 384 MiB of HBM per device.

```python
import jax
import jax.numpy as jnp
from jax import lax

H = 64
LAT = 512
DR = 64
DN = 128
DV = 128
D = 7168
BLOCK = 128
TOPK = 16
STEPS = 2
ROWS = 32
BLK_DEV = 16
NBLK = 1024
CTX = 131072
N_CTX = 64


def draw_query_rope(key, part):
    key = jax.random.fold_in(key, 7)
    key_noise = jax.random.fold_in(key, 1)
    values = jnp.clip(jax.random.normal(key_noise, (STEPS, ROWS, H, DR), jnp.float32), -6.0, 6.0)
    return values.reshape(STEPS, ROWS, H * DR).astype(jnp.bfloat16)


def draw_cache_rope(key, part):
    key = jax.random.fold_in(key, 9)
    values = jnp.clip(jax.random.normal(key, (CTX, DR), jnp.float32), -6.0, 6.0)
    return values.reshape(CTX // 2, 2 * DR).astype(jnp.bfloat16)


def draw_chosen_blocks(key, part):
    key = jax.random.fold_in(key, 5)
    total_picks = ROWS * TOPK
    capacity = 3 * total_picks // N_CTX
    hot_count = max(N_CTX // 8, 1)
    remaining = total_picks - hot_count * capacity
    other_count = N_CTX - hot_count
    base_load = remaining // other_count
    extra_count = remaining % other_count
    ranks = jnp.arange(N_CTX, dtype=jnp.int32)
    loads = jnp.where(ranks < hot_count, capacity, base_load + (ranks - hot_count < extra_count).astype(jnp.int32))
    load_ends = jnp.cumsum(loads).astype(jnp.int32)
    slots = jnp.arange(total_picks, dtype=jnp.int32)
    rank_of_slot = jnp.sum((slots[:, None] >= load_ends[None, :]).astype(jnp.int32), axis=1)
    earlier = jnp.arange(TOPK)[None, :] < jnp.arange(TOPK)[:, None]
    results = []
    for step_index in range(STEPS):
        step_key = jax.random.fold_in(key, step_index)
        key_devices, key_slots, key_base = jax.random.split(step_key, 3)
        device_of_rank = jax.random.permutation(key_devices, N_CTX).astype(jnp.int32)
        devices = device_of_rank[rank_of_slot]
        devices = devices[jax.random.permutation(key_slots, total_picks)].reshape(ROWS, TOPK)
        same_device = devices[:, :, None] == devices[:, None, :]
        repeat_rank = jnp.sum((same_device & earlier[None]).astype(jnp.int32), axis=2)
        base_offset = jax.random.randint(key_base, (ROWS, N_CTX), 0, BLK_DEV, dtype=jnp.int32)
        offsets = (jnp.take_along_axis(base_offset, devices, axis=1) + repeat_rank) % BLK_DEV
        results.append(devices * BLK_DEV + offsets)
    return jnp.stack(results, axis=0).astype(jnp.int32)


def shard_levels(key, dims, pieces, low, high):
    def one(dim, shards_of):
        heights = jax.random.uniform(jax.random.fold_in(jax.random.fold_in(key, 6), dim), (shards_of,), jnp.float32, low / len(pieces), high / len(pieces))
        return jnp.repeat(jnp.exp(heights), dims[dim] // shards_of).reshape((-1,) + (1,) * (len(dims) - dim - 1))

    gain = one(*pieces[0])
    for cut in pieces[1:]:
        gain = gain * one(*cut)
    return gain


def centred(own_key, extent, width, most, shards=(), kind=jnp.bfloat16):
    factor_of = shard_levels(own_key, extent, shards, -0.22, 0.18) if shards else 1.0
    drawn = jax.random.normal(own_key, extent, jnp.float32) * width * factor_of
    return jnp.minimum(jnp.maximum(drawn, -most), most).astype(kind)


def setup_inputs(seed: int = 0) -> dict:
    key_of = jax.random.split(jax.random.key(seed), 9)
    query_nope = centred(key_of[0], (STEPS, ROWS, H * DN), 2.0, 12.0, ((2, 4),))
    query_rope = draw_query_rope(jax.random.fold_in(key_of[8], 71), 0)
    key_up = centred(key_of[2], (H, DN, LAT), DN ** -0.5, 0.5, ((0, 4),))
    cache_latent = centred(key_of[3], (CTX, LAT), 1.0, 6.0, ((0, 64),))
    cache_rope = draw_cache_rope(jax.random.fold_in(key_of[8], 71), 0)
    chosen_blocks = draw_chosen_blocks(jax.random.fold_in(key_of[8], 71), 0)
    value_up = centred(key_of[6], (H, LAT, DV), LAT ** -0.5, 0.25, ((0, 4), (1, 64)))
    output_weight = centred(key_of[7], (H * DV, D), (H * DV // 16) ** -0.5, 0.25, ((0, 4), (1, 64)))
    return {"query_nope": query_nope, "query_rope": query_rope, "key_up": key_up, "cache_latent": cache_latent, "cache_rope": cache_rope, "chosen_blocks": chosen_blocks, "value_up": value_up, "output_weight": output_weight}


def reference(query_nope, query_rope, key_up, cache_latent, cache_rope, chosen_blocks, value_up, output_weight):
    score_scale = (DN + DR) ** -0.5
    latent_blocks = cache_latent.reshape(NBLK, BLOCK, LAT)
    rope_blocks = cache_rope.reshape(NBLK, BLOCK, DR)
    value_float = value_up.astype(jnp.float32)
    results = []
    for step_index in range(STEPS):
        nope_rows = query_nope[step_index].reshape(ROWS, H, DN).astype(jnp.float32)
        q_lat = jnp.einsum("rhn,hnl->rhl", nope_rows, key_up.astype(jnp.float32)).astype(jnp.bfloat16)
        rope_rows = query_rope[step_index].reshape(ROWS, H, DR).astype(jnp.float32)
        chosen = chosen_blocks[step_index]
        latent_sel = latent_blocks[chosen].astype(jnp.float32)
        rope_sel = rope_blocks[chosen].astype(jnp.float32)
        scores = jnp.einsum("rhl,rkbl->rhkb", q_lat.astype(jnp.float32), latent_sel)
        scores = (scores + jnp.einsum("rhd,rkbd->rhkb", rope_rows, rope_sel)) * score_scale
        block_peak = jnp.max(scores, axis=-1)
        shifted = jnp.exp(scores - block_peak[..., None])
        weights = shifted.astype(jnp.bfloat16)
        block_sum = jnp.sum(shifted, axis=-1)
        block_out = jnp.einsum("rhkb,rkbl->rhkl", weights.astype(jnp.float32), latent_sel)
        row_peak = jnp.max(block_peak, axis=-1)
        factor = jnp.exp(block_peak - row_peak[..., None])
        row_total = jnp.sum(factor * block_sum, axis=-1)
        merged = jnp.sum(factor[..., None] * block_out, axis=2)
        head_value = jnp.einsum("rhl,hlv->rhv", merged, value_float, precision=lax.Precision.HIGHEST)
        head_value = (head_value / row_total[..., None]).astype(jnp.bfloat16).reshape(ROWS, H * DV)
        results.append(jnp.dot(head_value, output_weight, preferred_element_type=jnp.float32).astype(jnp.bfloat16))
    return jnp.stack(results, axis=0)
```

```python
import functools

import jax
import jax.numpy as jnp
from jax import lax
from jax.experimental import pallas as pl
from jax.experimental.pallas import tpu as pltpu
from jax.sharding import Mesh
from jax.sharding import PartitionSpec as P

BLOCK = 128
LATENT = 512
HEADS = 16
ROWS = 32
ITEMS = HEADS * ROWS
ROW_STRIDE = 40
HEAD_STRIDE = 24
LANES = 128
UNROLL = 16
EARLY_ROWS = 8
PER_STEP = 16
PAIRS = 48
NONE = -1e30
MASKED = -3e38
F32 = jnp.float32
BF16 = jnp.bfloat16


def dot_t(a, b):
    return lax.dot_general(a, b, (((1,), (1,)), ((), ())), preferred_element_type=F32)


def dot(a, b):
    return jnp.dot(a, b, preferred_element_type=F32)


def split3(x):
    hi = x.astype(BF16).astype(F32)
    mid = (x - hi).astype(BF16).astype(F32)
    return hi, mid, x - hi - mid


def pack_stats(peak, total):
    lane = lax.broadcasted_iota(jnp.int32, peak.shape, 1) // 16
    parts = split3(peak) + split3(total)
    out = parts[0]
    for i in range(1, 6):
        out = jnp.where(lane == i, parts[i], out)
    return out.astype(BF16)


def spread_stats(packed, lanes_each):
    part = lax.broadcasted_iota(jnp.int32, (LANES, 2 * LANES), 0)
    side = lax.broadcasted_iota(jnp.int32, (LANES, 2 * LANES), 1) // LANES
    used = (part % 16 < lanes_each) & (part // 48 == side) & (part < 96)
    both = dot(packed, used.astype(BF16))
    return both[:, :LANES], both[:, LANES:]


def own_lanes(stats):
    lane = lax.broadcasted_iota(jnp.int32, stats.shape, 2) % 16
    return jnp.where(lane == lax.broadcasted_iota(jnp.int32, stats.shape, 1), stats, 0.0)


def attend_kernel(
    chosen_hbm, q_nope_hbm, q_rope_hbm, value_hbm, key_hbm, latent_hbm, rope_hbm, keep, send,
    chosen, acc, peak, total, q_nope, q_rope, key, latent, rope, q_lat, q_rot, rope_wide, scores, pairs, sems, *, scale
):
    core = lax.axis_index("core")
    device = (lax.axis_index("y") * 8 + lax.axis_index("z")) * 2 + core
    n_rows = 2 * ROWS
    copies = [
        pltpu.make_async_copy(src, dst, sems.at[i])
        for i, (src, dst) in enumerate(
            (
                (chosen_hbm, chosen),
                (q_nope_hbm, q_nope),
                (q_rope_hbm, q_rope),
                (rope_hbm, rope),
                (key_hbm, key),
                (latent_hbm, latent),
                (value_hbm, send.at[pl.ds(5 * ITEMS, LANES)]),
            )
        )
    ]
    for copy in copies:
        copy.start()

    copies[0].wait()

    def find(r, count):
        for s in range(2):
            offset = ((s ^ core) * ROWS + r) * 16 - device * 16
            for k in range(16):
                block = chosen[s, k, r]
                pairs[count] = block + offset
                count = count + ((block >> 4) == device).astype(jnp.int32)
        return count

    count = lax.fori_loop(0, EARLY_ROWS, find, jnp.int32(0))

    tok = lax.broadcasted_iota(jnp.int32, (BLOCK, BLOCK // 2), 0)
    pair = lax.broadcasted_iota(jnp.int32, (BLOCK, BLOCK // 2), 1)
    spread = (tok // 2 == pair).astype(BF16)
    half = (
        lax.broadcasted_iota(jnp.int32, (BLOCK, LANES), 1) // (LANES // 2)
        == lax.broadcasted_iota(jnp.int32, (BLOCK, LANES), 0) % 2
    )
    low = lax.broadcasted_iota(jnp.int32, (n_rows, LANES), 1) < LANES // 2

    late = (ROWS - EARLY_ROWS) * PER_STEP // HEADS

    def prepare(i, count):
        for u in range(late):
            count = find(EARLY_ROWS + i * late + u, count)
        for u in range(PER_STEP // 2):
            g = i * (PER_STEP // 2) + u
            two = q_rope[:, pl.ds(pl.multiple_of(g * LANES, LANES), LANES)].astype(F32)
            turned = pltpu.roll(two, LANES // 2, 1)
            q_rot[pl.ds(2 * g, n_rows, stride=HEAD_STRIDE), :] = jnp.where(low, two, turned)
            q_rot[pl.ds(2 * g + 1, n_rows, stride=HEAD_STRIDE), :] = jnp.where(low, turned, two)
        for u in range(PER_STEP):
            h = PER_STEP * i + u
            nope = q_nope[:, pl.ds(pl.multiple_of(h * LANES, LANES), LANES)]
            wide = dot(nope, key[h])
            for j in range(4):
                q_lat[j, pl.ds(h, n_rows, stride=HEAD_STRIDE), :] = wide[:, j * LANES : (j + 1) * LANES]
            keys = rope[pl.ds(pl.multiple_of(h * 64, 64), 64), :]
            there = pl.ds(pl.multiple_of(h * BLOCK, BLOCK), BLOCK)
            rope_wide[there, :] = jnp.where(half, dot(spread, keys), 0.0).astype(BF16)
        span = 2 * PER_STEP * ROW_STRIDE
        part = pl.ds(pl.multiple_of(i * span, span), span)
        for j in range(4):
            acc[j, part, :] = jnp.zeros((span, LANES), F32)
        total[part, :] = jnp.zeros((span, LANES), F32)
        peak[part, :] = jnp.full((span, LANES), NONE, F32)
        return count

    for copy in copies[1:5]:
        copy.wait()
    count = lax.fori_loop(0, HEADS // PER_STEP, prepare, count)
    for i in range(UNROLL):
        pairs[count + i] = 0
    chunks = (count + UNROLL - 1) // UNROLL
    copies[5].wait()

    def place(code):
        rel = code >> 4
        rel_step = rel >> 5
        row = rel & (ROWS - 1)
        first = pl.multiple_of(((rel_step ^ core) * ROWS + row) * HEAD_STRIDE, 8)
        where = pl.ds(rel_step * (HEADS * ROW_STRIDE) + row, HEADS, stride=ROW_STRIDE)
        tokens = pl.ds(pl.multiple_of((code & 15) * BLOCK, BLOCK), BLOCK)
        return pl.ds(first, HEADS), where, tokens

    def score(c, _):
        for u in range(UNROLL):
            p = c * UNROLL + u
            heads, where, tokens = place(pairs[p])
            query = jnp.concatenate([q_lat[j, heads, :] for j in range(4)], axis=1).astype(BF16)
            s = dot_t(latent[tokens, :], query) + dot_t(
                rope_wide[tokens, :], q_rot[heads, :].astype(BF16)
            )
            s = jnp.where(p < count, s.T * scale, MASKED)
            scores[p] = s
            peak[where, :] = jnp.maximum(peak[where, :], s)
        return 0

    lax.fori_loop(0, chunks, score, 0)
    for i in range(2 * HEADS):
        part = pl.ds(i * ROW_STRIDE, ROWS)
        peak[part, :] = jnp.broadcast_to(jnp.max(peak[part, :], axis=1, keepdims=True), (ROWS, LANES))

    def weigh(c, _):
        for u in range(UNROLL):
            p = c * UNROLL + u
            _, where, tokens = place(pairs[p])
            shifted = jnp.exp(scores[p] - peak[where, :])
            total[where, :] += shifted
            out = dot(shifted.astype(BF16), latent[tokens, :])
            for j in range(4):
                acc[j, where, :] += out[:, j * LANES : (j + 1) * LANES]
        return 0

    lax.fori_loop(0, chunks, weigh, 0)
    for i in range(2 * HEADS):
        part = pl.ds(i * ROW_STRIDE, ROWS)
        sums = jnp.broadcast_to(jnp.sum(total[part, :], axis=1, keepdims=True), (ROWS, LANES))
        there = [pl.ds(j * ITEMS + (i % HEADS) * ROWS, ROWS) for j in range(6)]
        if i < HEADS:
            for j in range(4):
                keep[there[j], :] = acc[j, part, :]
            keep[there[4], :] = peak[part, :]
            keep[there[5], :] = sums
        else:
            for j in range(4):
                send[there[j], :] = acc[j, part, :].astype(BF16)
            send[there[4], :] = pack_stats(peak[part, :], sums)
    copies[6].wait()


def gather_lanes(stats, copies):
    n = stats.shape[0] // 16
    kept = own_lanes(stats.astype(F32).reshape(n, 16, LANES)).reshape(n * 16, LANES).astype(BF16)
    row = lax.broadcasted_iota(jnp.int32, (n * copies, n * 16), 0) // copies
    item = lax.broadcasted_iota(jnp.int32, (n * copies, n * 16), 1) // 16
    return dot((row == item).astype(BF16), kept).astype(BF16)


def pair_kernel(keep, got, value, out0, out1, out2, out3, f1, f2, stats):
    core = lax.axis_index("core")
    me = lax.axis_index("y")
    n = 16
    m2, l2 = spread_stats(got[4 * ITEMS : 5 * ITEMS, :], 1)
    m1, l1 = keep[4 * ITEMS : 5 * ITEMS, :], keep[5 * ITEMS :, :]
    top = jnp.maximum(m1, m2)
    f1[...] = jnp.exp(m1 - top)
    f2[...] = jnp.exp(m2 - top)
    stats[...] = gather_lanes(pack_stats(top, l1 * f1[...] + l2 * f2[...]), 2).astype(F32)
    for k, out in enumerate((out0, out1, out2, out3)):
        to = (me + k) & 3
        for g in range(8):
            a = pl.ds(pl.multiple_of(to * 128 + g * n, n), n)
            for j in range(4):
                here = pl.ds(pl.multiple_of(j * ITEMS + to * 128 + g * n, n), n)
                both = keep[here, :] * f1[a, :] + got[here, :].astype(F32) * f2[a, :]
                out[g * 64 + j * n : g * 64 + (j + 1) * n, :] = both.astype(BF16)
        for i in range(2):
            own = value[pl.ds(pl.multiple_of(to * 32 + i * n, n), n), :].astype(F32)
            sib = got[pl.ds(pl.multiple_of(5 * ITEMS + to * 32 + i * n, n), n), :].astype(F32)
            first = jnp.where(core == 0, own, sib)
            second = jnp.where(core == 0, sib, own)
            for u in range(2):
                rows = slice(u * 8, u * 8 + 8)
                piece = jnp.concatenate([first[rows], second[rows]], axis=0).astype(BF16)
                at = 512 + (2 * i + u) * n
                out[at : at + n, :] = piece
        out[576:592, :] = stats[pl.ds(pl.multiple_of(to * 16, 16), 16), :].astype(BF16)


def cross_kernel(own, got1, got2, got3, out):
    me = lax.axis_index("y")
    n = 16
    sources = (own, got1, got2, got3)
    packed = []
    for src in sources:
        rows = src[576:592, :].astype(F32).reshape(8, 2, LANES)[:, :1]
        packed.append(own_lanes(jnp.broadcast_to(rows, (8, n, LANES))).reshape(128, LANES))
    tops, sums = spread_stats(jnp.concatenate(packed, axis=0).astype(BF16), n)
    tops, sums = tops.reshape(4, 128, LANES), sums.reshape(4, 128, LANES)
    top = jnp.max(tops, axis=0)
    factors = jnp.exp(tops - top[None])
    stats = pack_stats(top, jnp.sum(factors * sums, axis=0))
    out[:, 128:136, :] = gather_lanes(stats, 8).reshape(8, 8, LANES)
    for g in range(8):
        for j in range(4):
            here = slice(g * 64 + j * n, g * 64 + (j + 1) * n)
            total = jnp.zeros((n, LANES), F32)
            for k, src in enumerate(sources):
                total += src[here, :].astype(F32) * factors[k, g * n : (g + 1) * n]
            out[g, j * n : (j + 1) * n, :] = total.astype(BF16)
        for k, src in enumerate(sources):
            origin = (me + 4 - k) & 3
            at = 512 + (g // 2) * n
            out[g, pl.ds(pl.multiple_of(64 + origin * n, n), n), :] = src[at : at + n, :]


def merge_kernel(got, out):
    packed = got[:, 128:136, :].astype(F32)
    packed = own_lanes(jnp.concatenate([packed, packed], axis=1)).astype(BF16)
    tops, sums = (x.reshape(8, 16, LANES) for x in spread_stats(packed.reshape(128, LANES), 16))
    factors = jnp.exp(tops - jnp.max(tops, axis=0, keepdims=True))
    total = jnp.sum(factors * sums, axis=0)
    result = jnp.zeros((16, LANES), F32)
    for j in range(4):
        merged = jnp.sum(got[:, j * 16 : (j + 1) * 16, :].astype(F32) * factors, axis=0)
        value = got[:, 64 + j * 16 : 80 + j * 16, :].reshape(128, LANES)
        for part in split3(merged):
            result += dot(part.astype(BF16), value)
    result = (result / total).astype(BF16)
    for s in range(32):
        out[s] = result


def project_kernel(own, sib, weight, *outs):
    core = lax.axis_index("core")
    me = lax.axis_index("head")
    zero = core == 0
    total = jnp.zeros((2 * ROWS, weight.shape[0]), F32)
    for h in range(HEADS):
        mine = own[2 * h : 2 * h + 2].reshape(ROWS, LANES)
        other = sib[2 * h : 2 * h + 2].reshape(ROWS, LANES)
        rows = jnp.concatenate([jnp.where(zero, mine, other), jnp.where(zero, other, mine)], axis=0)
        total += dot_t(rows, weight[:, h * LANES : (h + 1) * LANES])
    total = total.reshape(2, 4, 8, weight.shape[0])
    for k in range(4):
        want = lax.rem(me + k, 4)
        part = total[:, 0]
        for i in range(1, 4):
            part = jnp.where(want == i, total[:, i], part)
        outs[k][...] = part


VMEM = pl.BlockSpec(memory_space=pltpu.VMEM)
SMEM = pl.BlockSpec(memory_space=pltpu.SMEM)
HBM = pl.BlockSpec(memory_space=pltpu.HBM)


def params(mebibytes=8):
    return pltpu.CompilerParams(vmem_limit_bytes=mebibytes * 1024 * 1024)


def body(
    query_nope, query_rope, key_up, cache_latent, cache_rope, chosen_blocks, value_up, output_weight
):
    steps, rows, _ = query_nope.shape
    heads, nope, latent = key_up.shape
    rot = cache_rope.shape[1] // 2
    scale = (nope + rot) ** (-0.5)
    swap = [(0, 1), (1, 0)]
    value = value_up.reshape(-1, LANES)
    n_rows = steps * rows
    keep, send = pl.pallas_call(
        functools.partial(attend_kernel, scale=scale),
        out_shape=(
            jax.ShapeDtypeStruct((6 * ITEMS, LANES), F32),
            jax.ShapeDtypeStruct((5 * ITEMS + value.shape[0], LANES), BF16),
        ),
        in_specs=[HBM] * 7,
        out_specs=(VMEM,) * 2,
        scratch_shapes=[
            pltpu.SMEM((steps, chosen_blocks.shape[2], rows), jnp.int32),
            pltpu.VMEM((4, steps * heads * ROW_STRIDE, LANES), F32),
            pltpu.VMEM((steps * heads * ROW_STRIDE, LANES), F32),
            pltpu.VMEM((steps * heads * ROW_STRIDE, LANES), F32),
            pltpu.VMEM((n_rows, heads * nope), BF16),
            pltpu.VMEM((n_rows, heads * rot), BF16),
            pltpu.VMEM(key_up.shape, BF16),
            pltpu.VMEM(cache_latent.shape, BF16),
            pltpu.VMEM(cache_rope.shape, BF16),
            pltpu.VMEM((4, n_rows * HEAD_STRIDE, LANES), F32),
            pltpu.VMEM((n_rows * HEAD_STRIDE, LANES), F32),
            pltpu.VMEM((cache_latent.shape[0], LANES), BF16),
            pltpu.VMEM((PAIRS + UNROLL, HEADS, LANES), F32),
            pltpu.SMEM((PAIRS + UNROLL,), jnp.int32),
            pltpu.SemaphoreType.DMA((7,)),
        ],
        compiler_params=params(40),
        name="attend",
    )(
        *(
            pltpu.with_memory_space_constraint(x, pltpu.HBM)
            for x in (
                chosen_blocks.transpose(0, 2, 1),
                query_nope.reshape(n_rows, -1),
                query_rope.reshape(n_rows, -1),
                value,
                key_up,
                cache_latent,
                cache_rope,
            )
        ),
    )
    got = lax.ppermute(send, "core", swap)
    blocks = pl.pallas_call(
        pair_kernel,
        out_shape=(jax.ShapeDtypeStruct((592, LANES), BF16),) * 4,
        in_specs=[VMEM] * 3,
        out_specs=(VMEM,) * 4,
        scratch_shapes=[
            pltpu.VMEM((ITEMS, LANES), F32),
            pltpu.VMEM((ITEMS, LANES), F32),
            pltpu.VMEM((64, LANES), F32),
        ],
        compiler_params=params(),
        name="pair",
    )(keep, got, value)
    got = [
        lax.ppermute(blocks[k], "y", [(i, (i + k) % 4) for i in range(4)]) for k in range(1, 4)
    ]
    packed = pl.pallas_call(
        cross_kernel,
        out_shape=jax.ShapeDtypeStruct((8, 136, LANES), BF16),
        in_specs=[VMEM] * 4,
        out_specs=VMEM,
        compiler_params=params(),
        name="cross",
    )(blocks[0], *got)
    parts = lax.all_to_all(packed, "z", 0, 0)
    values = pl.pallas_call(
        merge_kernel,
        out_shape=jax.ShapeDtypeStruct((32, 16, LANES), BF16),
        in_specs=[VMEM],
        out_specs=VMEM,
        compiler_params=params(),
        name="merge",
    )(parts)
    own = lax.all_to_all(values, ("y", "z"), 0, 0)
    sib = lax.ppermute(own, "core", swap)
    width = output_weight.shape[1]
    terms = pl.pallas_call(
        project_kernel,
        out_shape=(jax.ShapeDtypeStruct((steps, rows // 4, width), F32),) * 4,
        in_specs=[VMEM] * 3,
        out_specs=(VMEM,) * 4,
        compiler_params=params(),
        name="project",
    )(own, sib, output_weight.transpose(1, 0))
    out = terms[0]
    for k in range(1, 4):
        out = out + lax.ppermute(terms[k], "head", [(i, (i + k) % 4) for i in range(4)])
    return out.astype(BF16)


def solution(mesh):
    fine = Mesh(mesh.devices.reshape(4, 8, 2, 4), ("y", "z", "core", "head"))
    ctx = ("y", "z", "core")
    placed = (
        P(None, None, "head"),
        P(None, None, "head"),
        P("head", None, None),
        P(ctx, None),
        P(ctx, None),
        P(),
        P("head", ctx, None),
        P("head", ctx),
    )
    return jax.shard_map(
        body, mesh=fine, in_specs=placed, out_specs=P(None, "head", ctx), check_vma=False
    )
```

```python
import functools

import jax
import jax.numpy as jnp
from jax import lax
from jax.experimental import pallas as pl
from jax.experimental.pallas import tpu as pltpu
from jax.sharding import Mesh
from jax.sharding import PartitionSpec as P

BLOCK = 128
LATENT = 512
HEADS = 16
ROWS = 32
ITEMS = HEADS * ROWS
ROW_STRIDE = 40
HEAD_STRIDE = 24
LANES = 128
UNROLL = 8
PAIRS = 24
LIST = 64
NONE = -1e30
MASKED = -3e38
F32 = jnp.float32
BF16 = jnp.bfloat16


def dot_t(a, b):
    return lax.dot_general(a, b, (((1,), (1,)), ((), ())), preferred_element_type=F32)


def dot(a, b):
    return jnp.dot(a, b, preferred_element_type=F32)


def split3(x):
    hi = x.astype(BF16).astype(F32)
    mid = (x - hi).astype(BF16).astype(F32)
    return hi, mid, x - hi - mid


def pack_stats(peak, total):
    lane = lax.broadcasted_iota(jnp.int32, peak.shape, 1) // 16
    parts = split3(peak) + split3(total)
    out = parts[0]
    for i in range(1, 6):
        out = jnp.where(lane == i, parts[i], out)
    return out.astype(BF16)


def spread_stats(packed, lanes_each):
    part = lax.broadcasted_iota(jnp.int32, (LANES, 2 * LANES), 0)
    side = lax.broadcasted_iota(jnp.int32, (LANES, 2 * LANES), 1) // LANES
    used = (part % 16 < lanes_each) & (part // 48 == side) & (part < 96)
    both = dot(packed, used.astype(BF16))
    return both[:, :LANES], both[:, LANES:]


def own_lanes(stats):
    lane = lax.broadcasted_iota(jnp.int32, stats.shape, 2) % 16
    return jnp.where(lane == lax.broadcasted_iota(jnp.int32, stats.shape, 1), stats, 0.0)


def widen_rope(rope, rope_wide):
    tok = lax.broadcasted_iota(jnp.int32, (BLOCK, BLOCK // 2), 0)
    pair = lax.broadcasted_iota(jnp.int32, (BLOCK, BLOCK // 2), 1)
    spread = (tok // 2 == pair).astype(BF16)
    half = (
        lax.broadcasted_iota(jnp.int32, (BLOCK, LANES), 1) // (LANES // 2)
        == lax.broadcasted_iota(jnp.int32, (BLOCK, LANES), 0) % 2
    )
    for b in range(16):
        wide = dot(spread, rope[b * 64 : (b + 1) * 64, :])
        rope_wide[b * BLOCK : (b + 1) * BLOCK, :] = jnp.where(half, wide, 0.0).astype(BF16)


def place(code):
    row = code >> 4
    heads = pl.ds(pl.multiple_of(row * HEAD_STRIDE, 8), HEADS)
    where = pl.ds(row, HEADS, stride=ROW_STRIDE)
    tokens = pl.ds(pl.multiple_of((code & 15) * BLOCK, BLOCK), BLOCK)
    return heads, where, tokens


def chunks_of(count):
    return (count + UNROLL - 1) // UNROLL


def score_pairs(pairs, side, q_lat, q_rot, latent, rope_wide, scores, peak, scale):
    count = pairs[side, LIST - 1]

    def step(c, _):
        for u in range(UNROLL):
            p = c * UNROLL + u
            heads, where, tokens = place(pairs[side, p])
            query = jnp.concatenate([q_lat[j, heads, :] for j in range(4)], axis=1).astype(BF16)
            s = dot_t(latent[tokens, :], query) + dot_t(
                rope_wide[tokens, :], q_rot[heads, :].astype(BF16)
            )
            s = jnp.where(p < count, s.T * scale, MASKED)
            scores[p] = s
            peak[where, :] = jnp.maximum(peak[where, :], s)
        return 0

    lax.fori_loop(0, chunks_of(count), step, 0)


def prepare_kernel(
    chosen_hbm, q_nope_hbm, q_rope_hbm, key_hbm, latent_hbm, rope_hbm,
    q_lat, q_rot, scores, peak, latent, pairs,
    chosen, found, q_nope, q_rope, key, rope, rope_wide, sems, *, scale
):
    core = lax.axis_index("core")
    device = (lax.axis_index("y") * 8 + lax.axis_index("z")) * 2 + core
    mine = pl.ds(pl.multiple_of(core * ROWS, ROWS), ROWS)
    copies = [
        pltpu.make_async_copy(src, dst, sems.at[i])
        for i, (src, dst) in enumerate(
            (
                (chosen_hbm.at[core], chosen),
                (q_nope_hbm.at[mine], q_nope),
                (q_rope_hbm.at[mine], q_rope),
                (rope_hbm, rope),
                (key_hbm, key),
                (latent_hbm, latent),
            )
        )
    ]
    for copy in copies:
        copy.start()
    copies[0].wait()

    def find(r, count):
        offset = (r - (device >> 1)) * 32
        for k in range(16):
            block = chosen[k, r]
            found[count] = block + offset
            count = count + ((block >> 5) == (device >> 1)).astype(jnp.int32)
        return count

    def deal(p, counts):
        code = found[p]
        side = ((code >> 4) & 1) ^ core
        pairs[side, jnp.where(side == 0, counts[0], counts[1])] = ((code >> 5) << 4) + (code & 15)
        return counts[0] + (1 - side), counts[1] + side

    count = lax.fori_loop(0, 20, find, jnp.int32(0), unroll=2)
    for copy in copies[1:5]:
        copy.wait()
    for r in range(20, ROWS):
        count = find(r, count)
    low = lax.broadcasted_iota(jnp.int32, (ROWS, LANES), 1) < LANES // 2
    for g in range(HEADS // 2):
        two = q_rope[:, g * LANES : (g + 1) * LANES].astype(F32)
        turned = pltpu.roll(two, LANES // 2, 1)
        q_rot[pl.ds(2 * g, ROWS, stride=HEAD_STRIDE), :] = jnp.where(low, two, turned)
        q_rot[pl.ds(2 * g + 1, ROWS, stride=HEAD_STRIDE), :] = jnp.where(low, turned, two)
    for h in range(HEADS):
        wide = dot(q_nope[:, h * LANES : (h + 1) * LANES], key[h])
        for j in range(4):
            q_lat[j, pl.ds(h, ROWS, stride=HEAD_STRIDE), :] = wide[:, j * LANES : (j + 1) * LANES]
    widen_rope(rope, rope_wide)
    peak[...] = jnp.full_like(peak, NONE)
    counts = lax.fori_loop(0, count, deal, (jnp.int32(0), jnp.int32(0)))
    for side in range(2):
        for i in range(UNROLL):
            pairs[side, counts[side] + i] = 0
        pairs[side, LIST - 1] = counts[side]
    copies[5].wait()
    score_pairs(pairs, 0, q_lat, q_rot, latent, rope_wide, scores, peak, scale)


def gather_lanes(stats, copies):
    n = stats.shape[0] // 16
    kept = own_lanes(stats.astype(F32).reshape(n, 16, LANES)).reshape(n * 16, LANES).astype(BF16)
    row = lax.broadcasted_iota(jnp.int32, (n * copies, n * 16), 0) // copies
    item = lax.broadcasted_iota(jnp.int32, (n * copies, n * 16), 1) // 16
    return dot((row == item).astype(BF16), kept).astype(BF16)


def attend_kernel(
    pairs, q_lat, q_rot, scores, peak_own, latent, latent_sib, rope_sib, value, value_sib,
    out0, out1, out2, out3,
    rope_wide, scores_sib, peak, acc, total, stats, *, scale
):
    core = lax.axis_index("core")
    me = lax.axis_index("y")
    n = 16
    widen_rope(rope_sib, rope_wide)
    acc[...] = jnp.zeros_like(acc)
    total[...] = jnp.zeros_like(total)
    peak[...] = peak_own[...]
    score_pairs(pairs, 1, q_lat, q_rot, latent_sib, rope_wide, scores_sib, peak, scale)
    heads = [pl.ds(h * ROW_STRIDE, ROWS) for h in range(HEADS)]
    for part in heads:
        peak[part, :] = jnp.broadcast_to(jnp.max(peak[part, :], axis=1, keepdims=True), (ROWS, LANES))

    for side, (raw, keys) in enumerate(((scores, latent), (scores_sib, latent_sib))):

        def step(c, _):
            for u in range(UNROLL):
                p = c * UNROLL + u
                _, where, tokens = place(pairs[side, p])
                shifted = jnp.exp(raw[p] - peak[where, :])
                total[where, :] += shifted
                out = dot(shifted.astype(BF16), keys[tokens, :])
                for j in range(4):
                    acc[j, where, :] += out[:, j * LANES : (j + 1) * LANES]
            return 0

        lax.fori_loop(0, chunks_of(pairs[side, LIST - 1]), step, 0)

    tops = jnp.concatenate([peak[part, :] for part in heads], axis=0)
    sums = jnp.concatenate([total[part, :] for part in heads], axis=0)
    sums = jnp.broadcast_to(jnp.sum(sums, axis=1, keepdims=True), (ITEMS, LANES))
    stats[...] = gather_lanes(pack_stats(tops, sums), 2).astype(F32)
    for k, out in enumerate((out0, out1, out2, out3)):
        to = (me + k) & 3
        for g in range(8):
            first = to * (4 * ROW_STRIDE) + (g // 2) * ROW_STRIDE + (g % 2) * n
            here = pl.ds(pl.multiple_of(first, 8), n)
            for j in range(4):
                out[g * 64 + j * n : g * 64 + (j + 1) * n, :] = acc[j, here, :].astype(BF16)
        for i in range(2):
            here = pl.ds(pl.multiple_of(to * 32 + i * n, n), n)
            own, sib = value[here, :].astype(F32), value_sib[here, :].astype(F32)
            first = jnp.where(core == 0, own, sib)
            second = jnp.where(core == 0, sib, own)
            for u in range(2):
                rows = slice(u * 8, u * 8 + 8)
                piece = jnp.concatenate([first[rows], second[rows]], axis=0).astype(BF16)
                at = 512 + (2 * i + u) * n
                out[at : at + n, :] = piece
        out[576:592, :] = stats[pl.ds(pl.multiple_of(to * 16, 16), 16), :].astype(BF16)


def cross_kernel(own, got1, got2, got3, out):
    me = lax.axis_index("y")
    n = 16
    sources = (own, got1, got2, got3)
    packed = []
    for src in sources:
        rows = src[576:592, :].astype(F32).reshape(8, 2, LANES)[:, :1]
        packed.append(own_lanes(jnp.broadcast_to(rows, (8, n, LANES))).reshape(128, LANES))
    tops, sums = spread_stats(jnp.concatenate(packed, axis=0).astype(BF16), n)
    tops, sums = tops.reshape(4, 128, LANES), sums.reshape(4, 128, LANES)
    top = jnp.max(tops, axis=0)
    factors = jnp.exp(tops - top[None])
    stats = pack_stats(top, jnp.sum(factors * sums, axis=0))
    out[:, 128:136, :] = gather_lanes(stats, 8).reshape(8, 8, LANES)
    for g in range(8):
        for j in range(4):
            here = slice(g * 64 + j * n, g * 64 + (j + 1) * n)
            total = jnp.zeros((n, LANES), F32)
            for k, src in enumerate(sources):
                total += src[here, :].astype(F32) * factors[k, g * n : (g + 1) * n]
            out[g, j * n : (j + 1) * n, :] = total.astype(BF16)
        for k, src in enumerate(sources):
            origin = (me + 4 - k) & 3
            at = 512 + (g // 2) * n
            out[g, pl.ds(pl.multiple_of(64 + origin * n, n), n), :] = src[at : at + n, :]


def merge_kernel(got, out):
    packed = got[:, 128:136, :].astype(F32)
    packed = own_lanes(jnp.concatenate([packed, packed], axis=1)).astype(BF16)
    tops, sums = (x.reshape(8, 16, LANES) for x in spread_stats(packed.reshape(128, LANES), 16))
    factors = jnp.exp(tops - jnp.max(tops, axis=0, keepdims=True))
    total = jnp.sum(factors * sums, axis=0)
    result = jnp.zeros((16, LANES), F32)
    for j in range(4):
        merged = jnp.sum(got[:, j * 16 : (j + 1) * 16, :].astype(F32) * factors, axis=0)
        value = got[:, 64 + j * 16 : 80 + j * 16, :].reshape(128, LANES)
        for part in split3(merged):
            result += dot(part.astype(BF16), value)
    result = (result / total).astype(BF16)
    for s in range(32):
        out[s] = result


def project_kernel(own, sib, weight, *outs):
    core = lax.axis_index("core")
    me = lax.axis_index("head")
    zero = core == 0
    total = jnp.zeros((2 * ROWS, weight.shape[0]), F32)
    for h in range(HEADS):
        mine = own[2 * h : 2 * h + 2].reshape(ROWS, LANES)
        other = sib[2 * h : 2 * h + 2].reshape(ROWS, LANES)
        rows = jnp.concatenate([jnp.where(zero, mine, other), jnp.where(zero, other, mine)], axis=0)
        total += dot_t(rows, weight[:, h * LANES : (h + 1) * LANES])
    total = total.reshape(2, 4, 8, weight.shape[0])
    for k in range(4):
        want = lax.rem(me + k, 4)
        part = total[:, 0]
        for i in range(1, 4):
            part = jnp.where(want == i, total[:, i], part)
        outs[k][...] = part


VMEM = pl.BlockSpec(memory_space=pltpu.VMEM)
SMEM = pl.BlockSpec(memory_space=pltpu.SMEM)
HBM = pl.BlockSpec(memory_space=pltpu.HBM)


def params(mebibytes=8):
    return pltpu.CompilerParams(vmem_limit_bytes=mebibytes * 1024 * 1024)


def body(
    query_nope, query_rope, key_up, cache_latent, cache_rope, chosen_blocks, value_up, output_weight
):
    steps, rows, _ = query_nope.shape
    heads, nope, latent = key_up.shape
    rot = cache_rope.shape[1] // 2
    scale = (nope + rot) ** (-0.5)
    swap = [(0, 1), (1, 0)]
    value = value_up.reshape(-1, LANES)
    n_rows = steps * rows
    def from_sibling(x):
        return lax.ppermute(x, "core", swap)

    latent_sib, rope_sib, value_sib = (
        from_sibling(cache_latent),
        from_sibling(cache_rope),
        from_sibling(value),
    )
    slots = PAIRS + UNROLL
    q_lat, q_rot, scores, peak, latent_own, pairs = pl.pallas_call(
        functools.partial(prepare_kernel, scale=scale),
        out_shape=(
            jax.ShapeDtypeStruct((4, rows * HEAD_STRIDE, LANES), F32),
            jax.ShapeDtypeStruct((rows * HEAD_STRIDE, LANES), F32),
            jax.ShapeDtypeStruct((slots, heads, LANES), F32),
            jax.ShapeDtypeStruct((heads * ROW_STRIDE, LANES), F32),
            jax.ShapeDtypeStruct(cache_latent.shape, BF16),
            jax.ShapeDtypeStruct((2, LIST), jnp.int32),
        ),
        in_specs=[HBM] * 6,
        out_specs=(VMEM,) * 5 + (SMEM,),
        scratch_shapes=[
            pltpu.SMEM((chosen_blocks.shape[2], rows), jnp.int32),
            pltpu.SMEM((LIST,), jnp.int32),
            pltpu.VMEM((rows, heads * nope), BF16),
            pltpu.VMEM((rows, heads * rot), BF16),
            pltpu.VMEM(key_up.shape, BF16),
            pltpu.VMEM(cache_rope.shape, BF16),
            pltpu.VMEM((cache_latent.shape[0], LANES), BF16),
            pltpu.SemaphoreType.DMA((6,)),
        ],
        compiler_params=params(20),
        name="prepare",
    )(
        *(
            pltpu.with_memory_space_constraint(x, pltpu.HBM)
            for x in (
                chosen_blocks.transpose(0, 2, 1),
                query_nope.reshape(n_rows, -1),
                query_rope.reshape(n_rows, -1),
                key_up,
                cache_latent,
                cache_rope,
            )
        )
    )
    blocks = pl.pallas_call(
        functools.partial(attend_kernel, scale=scale),
        out_shape=(jax.ShapeDtypeStruct((592, LANES), BF16),) * 4,
        in_specs=[SMEM] + [VMEM] * 9,
        out_specs=(VMEM,) * 4,
        scratch_shapes=[
            pltpu.VMEM((cache_latent.shape[0], LANES), BF16),
            pltpu.VMEM((slots, heads, LANES), F32),
            pltpu.VMEM((heads * ROW_STRIDE, LANES), F32),
            pltpu.VMEM((4, heads * ROW_STRIDE, LANES), F32),
            pltpu.VMEM((heads * ROW_STRIDE, LANES), F32),
            pltpu.VMEM((64, LANES), F32),
        ],
        compiler_params=params(20),
        name="attend",
    )(pairs, q_lat, q_rot, scores, peak, latent_own, latent_sib, rope_sib, value, value_sib)
    got = [
        lax.ppermute(blocks[k], "y", [(i, (i + k) % 4) for i in range(4)]) for k in range(1, 4)
    ]
    packed = pl.pallas_call(
        cross_kernel,
        out_shape=jax.ShapeDtypeStruct((8, 136, LANES), BF16),
        in_specs=[VMEM] * 4,
        out_specs=VMEM,
        compiler_params=params(),
        name="cross",
    )(blocks[0], *got)
    parts = lax.all_to_all(packed, "z", 0, 0)
    values = pl.pallas_call(
        merge_kernel,
        out_shape=jax.ShapeDtypeStruct((32, 16, LANES), BF16),
        in_specs=[VMEM],
        out_specs=VMEM,
        compiler_params=params(),
        name="merge",
    )(parts)
    own = lax.all_to_all(values, ("y", "z"), 0, 0)
    sib = lax.ppermute(own, "core", swap)
    width = output_weight.shape[1]
    terms = pl.pallas_call(
        project_kernel,
        out_shape=(jax.ShapeDtypeStruct((steps, rows // 4, width), F32),) * 4,
        in_specs=[VMEM] * 3,
        out_specs=(VMEM,) * 4,
        compiler_params=params(),
        name="project",
    )(own, sib, output_weight.transpose(1, 0))
    out = terms[0]
    for k in range(1, 4):
        out = out + lax.ppermute(terms[k], "head", [(i, (i + k) % 4) for i in range(4)])
    return out.astype(BF16)


def solution(mesh):
    fine = Mesh(mesh.devices.reshape(4, 8, 2, 4), ("y", "z", "core", "head"))
    ctx = ("y", "z", "core")
    placed = (
        P(None, None, "head"),
        P(None, None, "head"),
        P("head", None, None),
        P(ctx, None),
        P(ctx, None),
        P(),
        P("head", ctx, None),
        P("head", ctx),
    )
    return jax.shard_map(
        body, mesh=fine, in_specs=placed, out_specs=P(None, "head", ctx), check_vma=False
    )
```

```python
import functools

import jax
import jax.numpy as jnp
from jax import lax
from jax.experimental import pallas as pl
from jax.experimental.pallas import tpu as pltpu
from jax.sharding import Mesh
from jax.sharding import PartitionSpec as P

BLOCK = 128
LATENT = 512
HEADS = 16
ROWS = 32
ITEMS = HEADS * ROWS
ROW_STRIDE = 40
HEAD_STRIDE = 24
LANES = 128
UNROLL = 12
PAIRS = 24
LIST = 64
NONE = -1e30
MASKED = -3e38
F32 = jnp.float32
BF16 = jnp.bfloat16


def dot_t(a, b):
    return lax.dot_general(a, b, (((1,), (1,)), ((), ())), preferred_element_type=F32)


def dot(a, b):
    return jnp.dot(a, b, preferred_element_type=F32)


def split3(x):
    hi = x.astype(BF16).astype(F32)
    mid = (x - hi).astype(BF16).astype(F32)
    return hi, mid, x - hi - mid


def pack_stats(peak, total):
    lane = lax.broadcasted_iota(jnp.int32, peak.shape, 1) // 16
    parts = split3(peak) + split3(total)
    out = parts[0]
    for i in range(1, 6):
        out = jnp.where(lane == i, parts[i], out)
    return out.astype(BF16)


def spread_stats(packed, lanes_each):
    part = lax.broadcasted_iota(jnp.int32, (LANES, 2 * LANES), 0)
    side = lax.broadcasted_iota(jnp.int32, (LANES, 2 * LANES), 1) // LANES
    used = (part % 16 < lanes_each) & (part // 48 == side) & (part < 96)
    both = dot(packed, used.astype(BF16))
    return both[:, :LANES], both[:, LANES:]


def own_lanes(stats):
    lane = lax.broadcasted_iota(jnp.int32, stats.shape, 2) % 16
    return jnp.where(lane == lax.broadcasted_iota(jnp.int32, stats.shape, 1), stats, 0.0)


def widen_rope(rope, rope_wide):
    tok = lax.broadcasted_iota(jnp.int32, (BLOCK, BLOCK // 2), 0)
    pair = lax.broadcasted_iota(jnp.int32, (BLOCK, BLOCK // 2), 1)
    spread = (tok // 2 == pair).astype(BF16)
    half = (
        lax.broadcasted_iota(jnp.int32, (BLOCK, LANES), 1) // (LANES // 2)
        == lax.broadcasted_iota(jnp.int32, (BLOCK, LANES), 0) % 2
    )
    for b in range(16):
        wide = dot(spread, rope[b * 64 : (b + 1) * 64, :])
        rope_wide[b * BLOCK : (b + 1) * BLOCK, :] = jnp.where(half, wide, 0.0).astype(BF16)


def place(code):
    row = code >> 4
    heads = pl.ds(pl.multiple_of(row * HEAD_STRIDE, 8), HEADS)
    where = pl.ds(row, HEADS, stride=ROW_STRIDE)
    tokens = pl.ds(pl.multiple_of((code & 15) * BLOCK, BLOCK), BLOCK)
    return heads, where, tokens


def chunks_of(count):
    return (count + UNROLL - 1) // UNROLL


def score_pairs(pairs, side, q_lat, q_rot, latent, rope_wide, scores, peak, scale):
    count = pairs[side, LIST - 1]

    def step(c, _):
        for u in range(UNROLL):
            p = c * UNROLL + u
            heads, where, tokens = place(pairs[side, p])
            query = jnp.concatenate([q_lat[j, heads, :] for j in range(4)], axis=1).astype(BF16)
            s = dot_t(latent[tokens, :], query) + dot_t(
                rope_wide[tokens, :], q_rot[heads, :].astype(BF16)
            )
            s = jnp.where(p < count, s.T * scale, MASKED)
            scores[p] = s
            peak[where, :] = jnp.maximum(peak[where, :], s)
        return 0

    lax.fori_loop(0, chunks_of(count), step, 0)


def prepare_kernel(
    chosen_hbm, q_nope_hbm, q_rope_hbm, key_hbm, latent_hbm, rope_hbm,
    q_lat, q_rot, scores, peak, latent, pairs,
    chosen, found, q_nope, q_rope, key, rope, rope_wide, sems, *, scale
):
    core = lax.axis_index("core")
    device = (lax.axis_index("y") * 8 + lax.axis_index("z")) * 2 + core
    mine = pl.ds(pl.multiple_of(core * ROWS, ROWS), ROWS)
    copies = [
        pltpu.make_async_copy(src, dst, sems.at[i])
        for i, (src, dst) in enumerate(
            (
                (chosen_hbm.at[core], chosen),
                (q_nope_hbm.at[mine], q_nope),
                (q_rope_hbm.at[mine], q_rope),
                (rope_hbm, rope),
                (key_hbm, key),
                (latent_hbm, latent),
            )
        )
    ]
    for copy in copies:
        copy.start()
    copies[0].wait()

    def find(r, count):
        offset = (r - (device >> 1)) * 32
        for k in range(16):
            block = chosen[k, r]
            found[count] = block + offset
            count = count + ((block >> 5) == (device >> 1)).astype(jnp.int32)
        return count

    def deal(p, counts):
        code = found[p]
        side = ((code >> 4) & 1) ^ core
        pairs[side, jnp.where(side == 0, counts[0], counts[1])] = ((code >> 5) << 4) + (code & 15)
        return counts[0] + (1 - side), counts[1] + side

    count = lax.fori_loop(0, 20, find, jnp.int32(0), unroll=2)
    for copy in copies[1:5]:
        copy.wait()
    for r in range(20, ROWS):
        count = find(r, count)
    low = lax.broadcasted_iota(jnp.int32, (ROWS, LANES), 1) < LANES // 2
    for g in range(HEADS // 2):
        two = q_rope[:, g * LANES : (g + 1) * LANES].astype(F32)
        turned = pltpu.roll(two, LANES // 2, 1)
        q_rot[pl.ds(2 * g, ROWS, stride=HEAD_STRIDE), :] = jnp.where(low, two, turned)
        q_rot[pl.ds(2 * g + 1, ROWS, stride=HEAD_STRIDE), :] = jnp.where(low, turned, two)
    for h in range(HEADS):
        wide = dot(q_nope[:, h * LANES : (h + 1) * LANES], key[h])
        for j in range(4):
            q_lat[j, pl.ds(h, ROWS, stride=HEAD_STRIDE), :] = wide[:, j * LANES : (j + 1) * LANES]
    widen_rope(rope, rope_wide)
    peak[...] = jnp.full_like(peak, NONE)
    counts = lax.fori_loop(0, count, deal, (jnp.int32(0), jnp.int32(0)))
    for side in range(2):
        for i in range(UNROLL):
            pairs[side, counts[side] + i] = 0
        pairs[side, LIST - 1] = counts[side]
    copies[5].wait()
    score_pairs(pairs, 0, q_lat, q_rot, latent, rope_wide, scores, peak, scale)


def gather_lanes(stats, copies):
    n = stats.shape[0] // 16
    kept = own_lanes(stats.astype(F32).reshape(n, 16, LANES)).reshape(n * 16, LANES).astype(BF16)
    row = lax.broadcasted_iota(jnp.int32, (n * copies, n * 16), 0) // copies
    item = lax.broadcasted_iota(jnp.int32, (n * copies, n * 16), 1) // 16
    return dot((row == item).astype(BF16), kept).astype(BF16)


def attend_kernel(
    pairs, q_lat, q_rot, scores, peak_own, latent, latent_sib, rope_sib, value, value_sib,
    out0, out1, out2, out3,
    rope_wide, scores_sib, peak, acc, total, stats, *, scale
):
    core = lax.axis_index("core")
    me = lax.axis_index("y")
    n = 16
    widen_rope(rope_sib, rope_wide)
    acc[...] = jnp.zeros_like(acc)
    total[...] = jnp.zeros_like(total)
    peak[...] = peak_own[...]
    score_pairs(pairs, 1, q_lat, q_rot, latent_sib, rope_wide, scores_sib, peak, scale)
    heads = [pl.ds(h * ROW_STRIDE, ROWS) for h in range(HEADS)]
    for part in heads:
        peak[part, :] = jnp.broadcast_to(jnp.max(peak[part, :], axis=1, keepdims=True), (ROWS, LANES))

    for side, (raw, keys) in enumerate(((scores, latent), (scores_sib, latent_sib))):

        def step(c, _):
            for u in range(UNROLL):
                p = c * UNROLL + u
                _, where, tokens = place(pairs[side, p])
                shifted = jnp.exp(raw[p] - peak[where, :])
                total[where, :] += shifted
                out = dot(shifted.astype(BF16), keys[tokens, :])
                for j in range(4):
                    acc[j, where, :] += out[:, j * LANES : (j + 1) * LANES]
            return 0

        lax.fori_loop(0, chunks_of(pairs[side, LIST - 1]), step, 0)

    tops = jnp.concatenate([peak[part, :] for part in heads], axis=0)
    sums = jnp.concatenate([total[part, :] for part in heads], axis=0)
    sums = jnp.broadcast_to(jnp.sum(sums, axis=1, keepdims=True), (ITEMS, LANES))
    stats[...] = gather_lanes(pack_stats(tops, sums), 2).astype(F32)
    for k, out in enumerate((out0, out1, out2, out3)):
        to = (me + k) & 3
        for g in range(8):
            first = to * (4 * ROW_STRIDE) + (g // 2) * ROW_STRIDE + (g % 2) * n
            here = pl.ds(pl.multiple_of(first, 8), n)
            for j in range(4):
                out[g * 64 + j * n : g * 64 + (j + 1) * n, :] = acc[j, here, :].astype(BF16)
        for i in range(2):
            here = pl.ds(pl.multiple_of(to * 32 + i * n, n), n)
            own, sib = value[here, :].astype(F32), value_sib[here, :].astype(F32)
            first = jnp.where(core == 0, own, sib)
            second = jnp.where(core == 0, sib, own)
            for u in range(2):
                rows = slice(u * 8, u * 8 + 8)
                piece = jnp.concatenate([first[rows], second[rows]], axis=0).astype(BF16)
                at = 512 + (2 * i + u) * n
                out[at : at + n, :] = piece
        out[576:592, :] = stats[pl.ds(pl.multiple_of(to * 16, 16), 16), :].astype(BF16)


def cross_kernel(own, got1, got2, got3, out):
    me = lax.axis_index("y")
    n = 16
    sources = (own, got1, got2, got3)
    packed = []
    for src in sources:
        rows = src[576:592, :].astype(F32).reshape(8, 2, LANES)[:, :1]
        packed.append(own_lanes(jnp.broadcast_to(rows, (8, n, LANES))).reshape(128, LANES))
    tops, sums = spread_stats(jnp.concatenate(packed, axis=0).astype(BF16), n)
    tops, sums = tops.reshape(4, 128, LANES), sums.reshape(4, 128, LANES)
    top = jnp.max(tops, axis=0)
    factors = jnp.exp(tops - top[None])
    stats = pack_stats(top, jnp.sum(factors * sums, axis=0))
    out[:, 128:136, :] = gather_lanes(stats, 8).reshape(8, 8, LANES)
    for g in range(8):
        for j in range(4):
            here = slice(g * 64 + j * n, g * 64 + (j + 1) * n)
            total = jnp.zeros((n, LANES), F32)
            for k, src in enumerate(sources):
                total += src[here, :].astype(F32) * factors[k, g * n : (g + 1) * n]
            out[g, j * n : (j + 1) * n, :] = total.astype(BF16)
        for k, src in enumerate(sources):
            origin = (me + 4 - k) & 3
            at = 512 + (g // 2) * n
            out[g, pl.ds(pl.multiple_of(64 + origin * n, n), n), :] = src[at : at + n, :]


def merge_kernel(got, out):
    packed = got[:, 128:136, :].astype(F32)
    packed = own_lanes(jnp.concatenate([packed, packed], axis=1)).astype(BF16)
    tops, sums = (x.reshape(8, 16, LANES) for x in spread_stats(packed.reshape(128, LANES), 16))
    factors = jnp.exp(tops - jnp.max(tops, axis=0, keepdims=True))
    total = jnp.sum(factors * sums, axis=0)
    result = jnp.zeros((16, LANES), F32)
    for j in range(4):
        merged = jnp.sum(got[:, j * 16 : (j + 1) * 16, :].astype(F32) * factors, axis=0)
        value = got[:, 64 + j * 16 : 80 + j * 16, :].reshape(128, LANES)
        for part in split3(merged):
            result += dot(part.astype(BF16), value)
    result = (result / total).astype(BF16)
    for s in range(32):
        out[s] = result


def project_kernel(own, sib, weight, *outs):
    core = lax.axis_index("core")
    me = lax.axis_index("head")
    zero = core == 0
    total = jnp.zeros((2 * ROWS, weight.shape[0]), F32)
    for h in range(HEADS):
        mine = own[2 * h : 2 * h + 2].reshape(ROWS, LANES)
        other = sib[2 * h : 2 * h + 2].reshape(ROWS, LANES)
        rows = jnp.concatenate([jnp.where(zero, mine, other), jnp.where(zero, other, mine)], axis=0)
        total += dot_t(rows, weight[:, h * LANES : (h + 1) * LANES])
    total = total.reshape(2, 4, 8, weight.shape[0])
    for k in range(4):
        want = lax.rem(me + k, 4)
        part = total[:, 0]
        for i in range(1, 4):
            part = jnp.where(want == i, total[:, i], part)
        outs[k][...] = part


VMEM = pl.BlockSpec(memory_space=pltpu.VMEM)
SMEM = pl.BlockSpec(memory_space=pltpu.SMEM)
HBM = pl.BlockSpec(memory_space=pltpu.HBM)


def params(mebibytes=8):
    return pltpu.CompilerParams(vmem_limit_bytes=mebibytes * 1024 * 1024)


def body(
    query_nope, query_rope, key_up, cache_latent, cache_rope, chosen_blocks, value_up, output_weight
):
    steps, rows, _ = query_nope.shape
    heads, nope, latent = key_up.shape
    rot = cache_rope.shape[1] // 2
    scale = (nope + rot) ** (-0.5)
    swap = [(0, 1), (1, 0)]
    value = value_up.reshape(-1, LANES)
    n_rows = steps * rows
    def from_sibling(x):
        return lax.ppermute(x, "core", swap)

    latent_sib, rope_sib, value_sib = (
        from_sibling(cache_latent),
        from_sibling(cache_rope),
        from_sibling(value),
    )
    slots = PAIRS + UNROLL
    q_lat, q_rot, scores, peak, latent_own, pairs = pl.pallas_call(
        functools.partial(prepare_kernel, scale=scale),
        out_shape=(
            jax.ShapeDtypeStruct((4, rows * HEAD_STRIDE, LANES), F32),
            jax.ShapeDtypeStruct((rows * HEAD_STRIDE, LANES), F32),
            jax.ShapeDtypeStruct((slots, heads, LANES), F32),
            jax.ShapeDtypeStruct((heads * ROW_STRIDE, LANES), F32),
            jax.ShapeDtypeStruct(cache_latent.shape, BF16),
            jax.ShapeDtypeStruct((2, LIST), jnp.int32),
        ),
        in_specs=[HBM] * 6,
        out_specs=(VMEM,) * 5 + (SMEM,),
        scratch_shapes=[
            pltpu.SMEM((chosen_blocks.shape[2], rows), jnp.int32),
            pltpu.SMEM((LIST,), jnp.int32),
            pltpu.VMEM((rows, heads * nope), BF16),
            pltpu.VMEM((rows, heads * rot), BF16),
            pltpu.VMEM(key_up.shape, BF16),
            pltpu.VMEM(cache_rope.shape, BF16),
            pltpu.VMEM((cache_latent.shape[0], LANES), BF16),
            pltpu.SemaphoreType.DMA((6,)),
        ],
        compiler_params=params(20),
        name="prepare",
    )(
        *(
            pltpu.with_memory_space_constraint(x, pltpu.HBM)
            for x in (
                chosen_blocks.transpose(0, 2, 1),
                query_nope.reshape(n_rows, -1),
                query_rope.reshape(n_rows, -1),
                key_up,
                cache_latent,
                cache_rope,
            )
        )
    )
    blocks = pl.pallas_call(
        functools.partial(attend_kernel, scale=scale),
        out_shape=(jax.ShapeDtypeStruct((592, LANES), BF16),) * 4,
        in_specs=[SMEM] + [VMEM] * 9,
        out_specs=(VMEM,) * 4,
        scratch_shapes=[
            pltpu.VMEM((cache_latent.shape[0], LANES), BF16),
            pltpu.VMEM((slots, heads, LANES), F32),
            pltpu.VMEM((heads * ROW_STRIDE, LANES), F32),
            pltpu.VMEM((4, heads * ROW_STRIDE, LANES), F32),
            pltpu.VMEM((heads * ROW_STRIDE, LANES), F32),
            pltpu.VMEM((64, LANES), F32),
        ],
        compiler_params=params(20),
        name="attend",
    )(pairs, q_lat, q_rot, scores, peak, latent_own, latent_sib, rope_sib, value, value_sib)
    got = {
        k: lax.ppermute(blocks[k], "y", [(i, (i + k) % 4) for i in range(4)]) for k in (2, 1, 3)
    }
    packed = pl.pallas_call(
        cross_kernel,
        out_shape=jax.ShapeDtypeStruct((8, 136, LANES), BF16),
        in_specs=[VMEM] * 4,
        out_specs=VMEM,
        compiler_params=params(),
        name="cross",
    )(blocks[0], got[1], got[2], got[3])
    parts = lax.all_to_all(packed, "z", 0, 0)
    values = pl.pallas_call(
        merge_kernel,
        out_shape=jax.ShapeDtypeStruct((32, 16, LANES), BF16),
        in_specs=[VMEM],
        out_specs=VMEM,
        compiler_params=params(),
        name="merge",
    )(parts)
    own = lax.all_to_all(values, ("y", "z"), 0, 0)
    sib = lax.ppermute(own, "core", swap)
    width = output_weight.shape[1]
    terms = pl.pallas_call(
        project_kernel,
        out_shape=(jax.ShapeDtypeStruct((steps, rows // 4, width), F32),) * 4,
        in_specs=[VMEM] * 3,
        out_specs=(VMEM,) * 4,
        compiler_params=params(),
        name="project",
    )(own, sib, output_weight.transpose(1, 0))
    out = terms[0]
    for k in range(1, 4):
        out = out + lax.ppermute(terms[k], "head", [(i, (i + k) % 4) for i in range(4)])
    return out.astype(BF16)


def solution(mesh):
    fine = Mesh(mesh.devices.reshape(4, 8, 2, 4), ("y", "z", "core", "head"))
    ctx = ("y", "z", "core")
    placed = (
        P(None, None, "head"),
        P(None, None, "head"),
        P("head", None, None),
        P(ctx, None),
        P(ctx, None),
        P(),
        P("head", ctx, None),
        P("head", ctx),
    )
    return jax.shard_map(
        body, mesh=fine, in_specs=placed, out_specs=P(None, "head", ctx), check_vma=False
    )
```

```python
import functools

import jax
import jax.numpy as jnp
from jax import lax
from jax.experimental import pallas as pl
from jax.experimental.pallas import tpu as pltpu
from jax.sharding import Mesh
from jax.sharding import PartitionSpec as P

BLOCK = 128
LATENT = 512
HEADS = 16
ROWS = 32
ITEMS = HEADS * ROWS
ROW_STRIDE = 40
HEAD_STRIDE = 24
LANES = 128
UNROLL = 12
PAIRS = 24
LIST = 64
NONE = -1e30
MASKED = -3e38
F32 = jnp.float32
BF16 = jnp.bfloat16


def dot_t(a, b):
    return lax.dot_general(a, b, (((1,), (1,)), ((), ())), preferred_element_type=F32)


def dot(a, b):
    return jnp.dot(a, b, preferred_element_type=F32)


def split3(x):
    hi = x.astype(BF16).astype(F32)
    mid = (x - hi).astype(BF16).astype(F32)
    return hi, mid, x - hi - mid


def pack_stats(peak, total):
    lane = lax.broadcasted_iota(jnp.int32, peak.shape, 1) // 16
    parts = split3(peak) + split3(total)
    out = parts[0]
    for i in range(1, 6):
        out = jnp.where(lane == i, parts[i], out)
    return out.astype(BF16)


def spread_stats(packed, lanes_each):
    part = lax.broadcasted_iota(jnp.int32, (LANES, 2 * LANES), 0)
    side = lax.broadcasted_iota(jnp.int32, (LANES, 2 * LANES), 1) // LANES
    used = (part % 16 < lanes_each) & (part // 48 == side) & (part < 96)
    both = dot(packed, used.astype(BF16))
    return both[:, :LANES], both[:, LANES:]


def own_lanes(stats):
    lane = lax.broadcasted_iota(jnp.int32, stats.shape, 2) % 16
    return jnp.where(lane == lax.broadcasted_iota(jnp.int32, stats.shape, 1), stats, 0.0)


def widen_rope(rope, rope_wide):
    tok = lax.broadcasted_iota(jnp.int32, (BLOCK, BLOCK // 2), 0)
    pair = lax.broadcasted_iota(jnp.int32, (BLOCK, BLOCK // 2), 1)
    spread = (tok // 2 == pair).astype(BF16)
    half = (
        lax.broadcasted_iota(jnp.int32, (BLOCK, LANES), 1) // (LANES // 2)
        == lax.broadcasted_iota(jnp.int32, (BLOCK, LANES), 0) % 2
    )
    for b in range(16):
        wide = dot(spread, rope[b * 64 : (b + 1) * 64, :])
        rope_wide[b * BLOCK : (b + 1) * BLOCK, :] = jnp.where(half, wide, 0.0).astype(BF16)


def place(code):
    row = code >> 4
    heads = pl.ds(pl.multiple_of(row * HEAD_STRIDE, 8), HEADS)
    where = pl.ds(row, HEADS, stride=ROW_STRIDE)
    tokens = pl.ds(pl.multiple_of((code & 15) * BLOCK, BLOCK), BLOCK)
    return heads, where, tokens


def chunks_of(count):
    return (count + UNROLL - 1) // UNROLL


def score_pairs(pairs, side, q_lat, q_rot, latent, rope_wide, scores, peak, scale):
    count = pairs[side, LIST - 1]

    def step(c, _):
        for u in range(UNROLL):
            p = c * UNROLL + u
            heads, where, tokens = place(pairs[side, p])
            query = jnp.concatenate([q_lat[j, heads, :] for j in range(4)], axis=1).astype(BF16)
            s = dot_t(latent[tokens, :], query) + dot_t(
                rope_wide[tokens, :], q_rot[heads, :].astype(BF16)
            )
            s = jnp.where(p < count, s.T * scale, MASKED)
            scores[p] = s
            peak[where, :] = jnp.maximum(peak[where, :], s)
        return 0

    step(0, 0)
    lax.fori_loop(1, chunks_of(count), step, 0)


def prepare_kernel(
    chosen_hbm, q_nope_hbm, q_rope_hbm, key_hbm, latent_hbm, rope_hbm,
    q_lat, q_rot, scores, peak, latent, pairs,
    chosen, found, q_nope, q_rope, key, rope, rope_wide, sems, *, scale
):
    core = lax.axis_index("core")
    device = (lax.axis_index("y") * 8 + lax.axis_index("z")) * 2 + core
    mine = pl.ds(pl.multiple_of(core * ROWS, ROWS), ROWS)
    copies = [
        pltpu.make_async_copy(src, dst, sems.at[i])
        for i, (src, dst) in enumerate(
            (
                (chosen_hbm.at[core], chosen),
                (q_nope_hbm.at[mine], q_nope),
                (q_rope_hbm.at[mine], q_rope),
                (rope_hbm, rope),
                (key_hbm, key),
                (latent_hbm, latent),
            )
        )
    ]
    for copy in copies:
        copy.start()
    copies[0].wait()

    def find(r, count):
        offset = (r - (device >> 1)) * 32
        for k in range(16):
            block = chosen[k, r]
            found[count] = block + offset
            count = count + ((block >> 5) == (device >> 1)).astype(jnp.int32)
        return count

    def deal(p, counts):
        code = found[p]
        side = ((code >> 4) & 1) ^ core
        pairs[side, jnp.where(side == 0, counts[0], counts[1])] = ((code >> 5) << 4) + (code & 15)
        return counts[0] + (1 - side), counts[1] + side

    count = lax.fori_loop(0, 20, find, jnp.int32(0), unroll=2)
    for copy in copies[1:5]:
        copy.wait()
    for r in range(20, ROWS):
        count = find(r, count)
    low = lax.broadcasted_iota(jnp.int32, (ROWS, LANES), 1) < LANES // 2
    for g in range(HEADS // 2):
        two = q_rope[:, g * LANES : (g + 1) * LANES].astype(F32)
        turned = pltpu.roll(two, LANES // 2, 1)
        q_rot[pl.ds(2 * g, ROWS, stride=HEAD_STRIDE), :] = jnp.where(low, two, turned)
        q_rot[pl.ds(2 * g + 1, ROWS, stride=HEAD_STRIDE), :] = jnp.where(low, turned, two)
    for h in range(HEADS):
        wide = dot(q_nope[:, h * LANES : (h + 1) * LANES], key[h])
        for j in range(4):
            q_lat[j, pl.ds(h, ROWS, stride=HEAD_STRIDE), :] = wide[:, j * LANES : (j + 1) * LANES]
    widen_rope(rope, rope_wide)
    peak[...] = jnp.full_like(peak, NONE)
    counts = lax.fori_loop(0, count, deal, (jnp.int32(0), jnp.int32(0)))
    for side in range(2):
        for i in range(UNROLL):
            pairs[side, counts[side] + i] = 0
        pairs[side, LIST - 1] = counts[side]
    copies[5].wait()
    score_pairs(pairs, 0, q_lat, q_rot, latent, rope_wide, scores, peak, scale)


def gather_lanes(stats, copies):
    n = stats.shape[0] // 16
    kept = own_lanes(stats.astype(F32).reshape(n, 16, LANES)).reshape(n * 16, LANES).astype(BF16)
    row = lax.broadcasted_iota(jnp.int32, (n * copies, n * 16), 0) // copies
    item = lax.broadcasted_iota(jnp.int32, (n * copies, n * 16), 1) // 16
    return dot((row == item).astype(BF16), kept).astype(BF16)


def attend_kernel(
    pairs, q_lat, q_rot, scores, peak_own, latent, latent_sib, rope_sib, value, value_sib,
    out0, out1, out2, out3,
    rope_wide, scores_sib, peak, acc, total, stats, *, scale
):
    core = lax.axis_index("core")
    me = lax.axis_index("y")
    n = 16
    widen_rope(rope_sib, rope_wide)
    acc[...] = jnp.zeros_like(acc)
    total[...] = jnp.zeros_like(total)
    peak[...] = peak_own[...]
    score_pairs(pairs, 1, q_lat, q_rot, latent_sib, rope_wide, scores_sib, peak, scale)
    heads = [pl.ds(h * ROW_STRIDE, ROWS) for h in range(HEADS)]
    for part in heads:
        peak[part, :] = jnp.broadcast_to(jnp.max(peak[part, :], axis=1, keepdims=True), (ROWS, LANES))

    def weigh(side, raw, keys, c):
        for u in range(UNROLL):
            p = c * UNROLL + u
            _, where, tokens = place(pairs[side, p])
            shifted = jnp.exp(raw[p] - peak[where, :])
            total[where, :] += shifted
            out = dot(shifted.astype(BF16), keys[tokens, :])
            for j in range(4):
                acc[j, where, :] += out[:, j * LANES : (j + 1) * LANES]

    sides = ((0, scores, latent), (1, scores_sib, latent_sib))
    for side, raw, keys in sides:
        weigh(side, raw, keys, 0)
    for side, raw, keys in sides:

        def step(c, _, side=side, raw=raw, keys=keys):
            weigh(side, raw, keys, c)
            return 0

        lax.fori_loop(1, chunks_of(pairs[side, LIST - 1]), step, 0)

    tops = jnp.concatenate([peak[part, :] for part in heads], axis=0)
    sums = jnp.concatenate([total[part, :] for part in heads], axis=0)
    sums = jnp.broadcast_to(jnp.sum(sums, axis=1, keepdims=True), (ITEMS, LANES))
    stats[...] = gather_lanes(pack_stats(tops, sums), 2).astype(F32)
    for k, out in enumerate((out0, out1, out2, out3)):
        to = (me + k) & 3
        for g in range(8):
            first = to * (4 * ROW_STRIDE) + (g // 2) * ROW_STRIDE + (g % 2) * n
            here = pl.ds(pl.multiple_of(first, 8), n)
            for j in range(4):
                out[g * 64 + j * n : g * 64 + (j + 1) * n, :] = acc[j, here, :].astype(BF16)
        for i in range(2):
            here = pl.ds(pl.multiple_of(to * 32 + i * n, n), n)
            own, sib = value[here, :].astype(F32), value_sib[here, :].astype(F32)
            first = jnp.where(core == 0, own, sib)
            second = jnp.where(core == 0, sib, own)
            for u in range(2):
                rows = slice(u * 8, u * 8 + 8)
                piece = jnp.concatenate([first[rows], second[rows]], axis=0).astype(BF16)
                at = 512 + (2 * i + u) * n
                out[at : at + n, :] = piece
        out[576:592, :] = stats[pl.ds(pl.multiple_of(to * 16, 16), 16), :].astype(BF16)


def cross_kernel(own, got1, got2, got3, out):
    me = lax.axis_index("y")
    n = 16
    sources = (own, got1, got2, got3)
    packed = []
    for src in sources:
        rows = src[576:592, :].astype(F32).reshape(8, 2, LANES)[:, :1]
        packed.append(own_lanes(jnp.broadcast_to(rows, (8, n, LANES))).reshape(128, LANES))
    tops, sums = spread_stats(jnp.concatenate(packed, axis=0).astype(BF16), n)
    tops, sums = tops.reshape(4, 128, LANES), sums.reshape(4, 128, LANES)
    top = jnp.max(tops, axis=0)
    factors = jnp.exp(tops - top[None])
    stats = pack_stats(top, jnp.sum(factors * sums, axis=0))
    out[:, 128:136, :] = gather_lanes(stats, 8).reshape(8, 8, LANES)
    for g in range(8):
        for j in range(4):
            here = slice(g * 64 + j * n, g * 64 + (j + 1) * n)
            total = jnp.zeros((n, LANES), F32)
            for k, src in enumerate(sources):
                total += src[here, :].astype(F32) * factors[k, g * n : (g + 1) * n]
            out[g, j * n : (j + 1) * n, :] = total.astype(BF16)
        for k, src in enumerate(sources):
            origin = (me + 4 - k) & 3
            at = 512 + (g // 2) * n
            out[g, pl.ds(pl.multiple_of(64 + origin * n, n), n), :] = src[at : at + n, :]


def merge_kernel(got, out):
    packed = got[:, 128:136, :].astype(F32)
    packed = own_lanes(jnp.concatenate([packed, packed], axis=1)).astype(BF16)
    tops, sums = (x.reshape(8, 16, LANES) for x in spread_stats(packed.reshape(128, LANES), 16))
    factors = jnp.exp(tops - jnp.max(tops, axis=0, keepdims=True))
    total = jnp.sum(factors * sums, axis=0)
    result = jnp.zeros((16, LANES), F32)
    for j in range(4):
        merged = jnp.sum(got[:, j * 16 : (j + 1) * 16, :].astype(F32) * factors, axis=0)
        value = got[:, 64 + j * 16 : 80 + j * 16, :].reshape(128, LANES)
        for part in split3(merged):
            result += dot(part.astype(BF16), value)
    result = (result / total).astype(BF16)
    for s in range(32):
        out[s] = result


def project_kernel(own, sib, weight, *outs):
    core = lax.axis_index("core")
    me = lax.axis_index("head")
    zero = core == 0
    total = jnp.zeros((2 * ROWS, weight.shape[0]), F32)
    for h in range(HEADS):
        mine = own[2 * h : 2 * h + 2].reshape(ROWS, LANES)
        other = sib[2 * h : 2 * h + 2].reshape(ROWS, LANES)
        rows = jnp.concatenate([jnp.where(zero, mine, other), jnp.where(zero, other, mine)], axis=0)
        total += dot_t(rows, weight[:, h * LANES : (h + 1) * LANES])
    total = total.reshape(2, 4, 8, weight.shape[0])
    for k in range(4):
        want = lax.rem(me + k, 4)
        part = total[:, 0]
        for i in range(1, 4):
            part = jnp.where(want == i, total[:, i], part)
        outs[k][...] = part


VMEM = pl.BlockSpec(memory_space=pltpu.VMEM)
SMEM = pl.BlockSpec(memory_space=pltpu.SMEM)
HBM = pl.BlockSpec(memory_space=pltpu.HBM)


def params(mebibytes=8):
    return pltpu.CompilerParams(vmem_limit_bytes=mebibytes * 1024 * 1024)


def body(
    query_nope, query_rope, key_up, cache_latent, cache_rope, chosen_blocks, value_up, output_weight
):
    steps, rows, _ = query_nope.shape
    heads, nope, latent = key_up.shape
    rot = cache_rope.shape[1] // 2
    scale = (nope + rot) ** (-0.5)
    swap = [(0, 1), (1, 0)]
    value = value_up.reshape(-1, LANES)
    n_rows = steps * rows
    def from_sibling(x):
        return lax.ppermute(x, "core", swap)

    latent_sib, rope_sib, value_sib = (
        from_sibling(cache_latent),
        from_sibling(cache_rope),
        from_sibling(value),
    )
    slots = PAIRS + UNROLL
    q_lat, q_rot, scores, peak, latent_own, pairs = pl.pallas_call(
        functools.partial(prepare_kernel, scale=scale),
        out_shape=(
            jax.ShapeDtypeStruct((4, rows * HEAD_STRIDE, LANES), F32),
            jax.ShapeDtypeStruct((rows * HEAD_STRIDE, LANES), F32),
            jax.ShapeDtypeStruct((slots, heads, LANES), F32),
            jax.ShapeDtypeStruct((heads * ROW_STRIDE, LANES), F32),
            jax.ShapeDtypeStruct(cache_latent.shape, BF16),
            jax.ShapeDtypeStruct((2, LIST), jnp.int32),
        ),
        in_specs=[HBM] * 6,
        out_specs=(VMEM,) * 5 + (SMEM,),
        scratch_shapes=[
            pltpu.SMEM((chosen_blocks.shape[2], rows), jnp.int32),
            pltpu.SMEM((LIST,), jnp.int32),
            pltpu.VMEM((rows, heads * nope), BF16),
            pltpu.VMEM((rows, heads * rot), BF16),
            pltpu.VMEM(key_up.shape, BF16),
            pltpu.VMEM(cache_rope.shape, BF16),
            pltpu.VMEM((cache_latent.shape[0], LANES), BF16),
            pltpu.SemaphoreType.DMA((6,)),
        ],
        compiler_params=params(20),
        name="prepare",
    )(
        *(
            pltpu.with_memory_space_constraint(x, pltpu.HBM)
            for x in (
                chosen_blocks.transpose(0, 2, 1),
                query_nope.reshape(n_rows, -1),
                query_rope.reshape(n_rows, -1),
                key_up,
                cache_latent,
                cache_rope,
            )
        )
    )
    blocks = pl.pallas_call(
        functools.partial(attend_kernel, scale=scale),
        out_shape=(jax.ShapeDtypeStruct((592, LANES), BF16),) * 4,
        in_specs=[SMEM] + [VMEM] * 9,
        out_specs=(VMEM,) * 4,
        scratch_shapes=[
            pltpu.VMEM((cache_latent.shape[0], LANES), BF16),
            pltpu.VMEM((slots, heads, LANES), F32),
            pltpu.VMEM((heads * ROW_STRIDE, LANES), F32),
            pltpu.VMEM((4, heads * ROW_STRIDE, LANES), F32),
            pltpu.VMEM((heads * ROW_STRIDE, LANES), F32),
            pltpu.VMEM((64, LANES), F32),
        ],
        compiler_params=params(20),
        name="attend",
    )(pairs, q_lat, q_rot, scores, peak, latent_own, latent_sib, rope_sib, value, value_sib)
    got = {
        k: lax.ppermute(blocks[k], "y", [(i, (i + k) % 4) for i in range(4)]) for k in (2, 1, 3)
    }
    packed = pl.pallas_call(
        cross_kernel,
        out_shape=jax.ShapeDtypeStruct((8, 136, LANES), BF16),
        in_specs=[VMEM] * 4,
        out_specs=VMEM,
        compiler_params=params(),
        name="cross",
    )(blocks[0], got[1], got[2], got[3])
    parts = lax.all_to_all(packed, "z", 0, 0)
    values = pl.pallas_call(
        merge_kernel,
        out_shape=jax.ShapeDtypeStruct((32, 16, LANES), BF16),
        in_specs=[VMEM],
        out_specs=VMEM,
        compiler_params=params(),
        name="merge",
    )(parts)
    own = lax.all_to_all(values, ("y", "z"), 0, 0)
    sib = lax.ppermute(own, "core", swap)
    width = output_weight.shape[1]
    terms = pl.pallas_call(
        project_kernel,
        out_shape=(jax.ShapeDtypeStruct((steps, rows // 4, width), F32),) * 4,
        in_specs=[VMEM] * 3,
        out_specs=(VMEM,) * 4,
        compiler_params=params(),
        name="project",
    )(own, sib, output_weight.transpose(1, 0))
    out = terms[0]
    for k in range(1, 4):
        out = out + lax.ppermute(terms[k], "head", [(i, (i + k) % 4) for i in range(4)])
    return out.astype(BF16)


def solution(mesh):
    fine = Mesh(mesh.devices.reshape(4, 8, 2, 4), ("y", "z", "core", "head"))
    ctx = ("y", "z", "core")
    placed = (
        P(None, None, "head"),
        P(None, None, "head"),
        P("head", None, None),
        P(ctx, None),
        P(ctx, None),
        P(),
        P("head", ctx, None),
        P("head", ctx),
    )
    return jax.shard_map(
        body, mesh=fine, in_specs=placed, out_specs=P(None, "head", ctx), check_vma=False
    )
```
